32 devices in a mesh: head: 8 (over z, y), ctx: 4 (over x, core).
Axes of the slice: x: 2, y: 2, z: 4, core: 2. Of those that a mesh axis runs over, the one named last changes fastest.
Arguments:
- queries: bfloat16 [64, 24576], P(('head', 'ctx')), may hold values from -5 to 5
- w_uk: bfloat16 [128, 128, 512], P('head'), may hold values from -0.5 to 0.5
- w_uv: bfloat16 [128, 512, 128], P('head'), may hold values from -0.25 to 0.25
- latent_cache: bfloat16 [512, 576], P('ctx'), may hold values from -8 to 8
- span_offset: int32 [1], replicated, may hold values from 0 to 448
Outputs:
- head_outputs: bfloat16 [64, 16384], P(('head', 'ctx'))
The draws below stay inside these ranges and needn't reach their ends.
Inputs may be any that keep to these rules, and one draw needn't show every extreme that they name: The span's latents are in the cache at positions span_offset to span_offset + 63.
All inputs are finite; a program needn't handle non-finite values.
Results may differ from the reference program's by a relative error of at most 0.0071.
Values may be sent and summed in bfloat16 or wider, within the bound.
A program may use at most 64 MiB of HBM per device.

```python
import math
import jax
import jax.numpy as jnp
from jax import lax

H = 128
NOPE = 128
ROPE = 64
LATENT = 512
VDIM = 128
SPAN = 64
CACHE = 512


def draw_queries(key, part):
    shape_here = (SPAN, H, NOPE + ROPE)
    entries = jnp.clip(jax.random.normal(jax.random.fold_in(key, 11), shape_here, jnp.float32), -5.0, 5.0)
    return entries.reshape(SPAN, H * (NOPE + ROPE)).astype(jnp.bfloat16)


def draw_latent_cache(key, part):
    shape_here = (CACHE, LATENT + ROPE)
    entries = jnp.clip(0.8 * jax.random.normal(jax.random.fold_in(key, 23), shape_here, jnp.float32), -4.0, 4.0)
    return entries.astype(jnp.bfloat16)


def block_levels(key, extent, shards, low, largest):
    def one(dim, blocks):
        draws = jax.random.uniform(jax.random.fold_in(jax.random.fold_in(key, 6), dim), (blocks,), jnp.float32, low / len(shards), largest / len(shards))
        return jnp.repeat(jnp.exp(draws), extent[dim] // blocks).reshape((-1,) + (1,) * (len(extent) - dim - 1))

    gain = one(*shards[0])
    for cut in shards[1:]:
        gain = gain * one(*cut)
    return gain


def centred(rng, shape, width, limit, cuts=(), held_as=jnp.bfloat16):
    values = width * jax.random.normal(rng, shape, jnp.float32)
    if cuts:
        values = values * block_levels(rng, shape, cuts, -0.22, 0.18)
    return jnp.clip(values, -limit, limit).astype(held_as)


def setup_inputs(seed: int = 0) -> dict:
    key_list = jax.random.split(jax.random.key(seed), 6)
    return {
        "queries": draw_queries(jax.random.fold_in(key_list[5], 71), 0),
        "w_uk": centred(key_list[1], (H, NOPE, LATENT), NOPE ** -0.5, 0.5, ((0, 8),)),
        "w_uv": centred(key_list[2], (H, LATENT, VDIM), LATENT ** -0.5, 0.25, ((0, 8),)),
        "latent_cache": draw_latent_cache(jax.random.fold_in(key_list[5], 71), 0),
        "span_offset": jax.random.randint(key_list[4], (1,), 0, CACHE - SPAN + 1).astype(jnp.int32),
    }


yarn_mscale = 0.1 * math.log(40.0) + 1.0


def reference(queries, w_uk, w_uv, latent_cache, span_offset):
    query_width = NOPE + ROPE
    shaped = queries.reshape(SPAN, H, query_width)
    q_lat = jnp.einsum("thn,hnl->thl", shaped[:, :, :NOPE].astype(jnp.float32), w_uk.astype(jnp.float32)).astype(jnp.bfloat16)
    q_all = jnp.concatenate([q_lat, shaped[:, :, NOPE:]], axis=2)
    score_scale = query_width ** -0.5 * yarn_mscale ** 2
    query_pos = span_offset[0] + jnp.arange(SPAN, dtype=jnp.int32)
    key_slots = jnp.arange(CACHE, dtype=jnp.int32)
    visible = key_slots[None, :] <= query_pos[:, None]
    latent_values = latent_cache[:, :LATENT]

    def one_head(inputs):
        query_head, weight_head = inputs
        scores = jnp.dot(query_head, latent_cache.T, preferred_element_type=jnp.float32) * score_scale
        scores = jnp.where(visible, scores, -jnp.inf)
        row_top = jnp.max(scores, axis=1, keepdims=True)
        expo = jnp.exp(scores - row_top)
        total = jnp.sum(expo, axis=1, keepdims=True)
        weights = expo.astype(jnp.bfloat16)
        attended = (jnp.dot(weights, latent_values, preferred_element_type=jnp.float32) / total).astype(jnp.bfloat16)
        return jnp.dot(attended, weight_head, preferred_element_type=jnp.float32).astype(jnp.bfloat16)

    per_head = lax.map(one_head, (jnp.transpose(q_all, (1, 0, 2)), w_uv))
    return jnp.transpose(per_head, (1, 0, 2)).reshape(SPAN, H * VDIM)
```

```python
import functools
import math

import jax
import jax.numpy as jnp
from jax import lax
from jax.experimental import pallas as pl
from jax.experimental.pallas import tpu as pltpu
from jax.sharding import PartitionSpec as P

NOPE = 128
ROPE = 64
LATENT = 512
VDIM = 128
WIDTH = NOPE + ROPE
MESH = pl.DeviceIdType.MESH

yarn_mscale = 0.1 * math.log(40.0) + 1.0
score_scale = WIDTH ** (-0.5) * yarn_mscale**2


def kernel(
    n_head, n_ctx, q_hbm, uk_hbm, uv_hbm, cache_hbm, offset_ref, out_ref,
    q_in, q_got, q_rows, uk, uv, q_all, cache, scores, acc, heads_out, slabs,
    local_sem, q_send, q_recv, own_send, fwd_send, cache_recv, o_send, o_recv,
):
    tokens = q_hbm.shape[0]
    heads = uk_hbm.shape[0]
    span = cache_hbm.shape[0]
    chips = n_ctx // 2
    all_tokens = n_head * tokens
    rows = heads * all_tokens
    q_cols = heads * WIDTH
    o_cols = heads * VDIM
    h_me = lax.axis_index("head")
    c_me = lax.axis_index("ctx")
    chip = c_me // 2
    core = c_me % 2
    sibling = chip * 2 + 1 - core

    def head_peer(i):
        return lax.rem(h_me + i, n_head)

    def chip_peer(i):
        return lax.rem(chip + i, chips)

    def piece(chip_at, core_at):
        return cache.at[chip_at, pl.ds(pl.multiple_of(core_at * span, span), span), :]

    load_q = pltpu.make_async_copy(q_hbm, q_in, local_sem.at[0])
    load_cache = pltpu.make_async_copy(cache_hbm, piece(chip, core), local_sem.at[1])
    load_uk = pltpu.make_async_copy(uk_hbm, uk, local_sem.at[2])
    load_uv = pltpu.make_async_copy(uv_hbm, uv, local_sem.at[3])
    load_q.start()
    load_cache.start()
    load_uk.start()
    load_uv.start()

    barrier = pltpu.get_barrier_semaphore()
    for i in range(1, n_head):
        pl.semaphore_signal(barrier, inc=1, device_id=(head_peer(i), c_me), device_id_type=MESH)
    for i in range(1, chips):
        pl.semaphore_signal(
            barrier, inc=1, device_id=(h_me, chip_peer(i) * 2 + core), device_id_type=MESH
        )
    pl.semaphore_signal(barrier, inc=1, device_id=(h_me, sibling), device_id_type=MESH)
    load_q.wait()
    load_cache.wait()
    pl.semaphore_wait(barrier, n_head - 1 + chips)

    cache_far = []
    for i in range(1, chips):
        there = chip_peer(i)
        copy = pltpu.make_async_remote_copy(
            src_ref=piece(chip, core),
            dst_ref=piece(chip, core),
            send_sem=own_send.at[i],
            recv_sem=cache_recv.at[chip, core],
            device_id=(h_me, there * 2 + core),
            device_id_type=MESH,
        )
        copy.start()
        cache_far.append(copy)
    q_copies = []
    for i in range(1, n_head):
        there = head_peer(i)
        copy = pltpu.make_async_remote_copy(
            src_ref=q_in.at[:, pl.ds(pl.multiple_of(there * q_cols, 128), q_cols)],
            dst_ref=q_got.at[h_me],
            send_sem=q_send.at[i],
            recv_sem=q_recv.at[h_me],
            device_id=(there, c_me),
            device_id_type=MESH,
        )
        copy.start()
        q_copies.append(copy)
    to_sibling = pltpu.make_async_remote_copy(
        src_ref=piece(chip, core),
        dst_ref=piece(chip, core),
        send_sem=own_send.at[0],
        recv_sem=cache_recv.at[chip, core],
        device_id=(h_me, sibling),
        device_id_type=MESH,
    )
    to_sibling.start()
    own_q = pltpu.make_async_copy(
        q_in.at[:, pl.ds(pl.multiple_of(h_me * q_cols, 128), q_cols)],
        q_got.at[h_me],
        local_sem.at[4],
    )
    own_q.start()
    own_q.wait()

    def arrival(sem, dst, src=None):
        return pltpu.make_async_remote_copy(
            src_ref=dst,
            dst_ref=dst,
            send_sem=sem,
            recv_sem=sem,
            device_id=(h_me, sibling),
            device_id_type=MESH,
        )

    for i in range(1, n_head):
        there = head_peer(i)
        arrival(q_recv.at[there], q_got.at[there]).wait_recv()
    for p in range(n_head):
        q_rows[p * tokens : (p + 1) * tokens, :] = q_got[p].astype(jnp.float32)
    load_uk.wait()
    for pair in range(heads // 2):
        both = q_rows[:, pair * 2 * WIDTH : (pair + 1) * 2 * WIDTH].astype(jnp.bfloat16)
        for k in range(2):
            h = pair * 2 + k
            at = pl.ds(h * all_tokens, all_tokens)
            plain = both[:, k * WIDTH : k * WIDTH + NOPE]
            turned = both[:, k * WIDTH + NOPE : (k + 1) * WIDTH]
            q_all[at, :LATENT] = jnp.dot(
                plain, uk[h], preferred_element_type=jnp.float32
            ).astype(jnp.bfloat16)
            q_all[at, LATENT:] = turned

    forwards = []
    for i in range(1, chips):
        there = chip_peer(i)
        arrival(cache_recv.at[there, core], piece(there, core)).wait_recv()
        copy = pltpu.make_async_remote_copy(
            src_ref=piece(there, core),
            dst_ref=piece(there, core),
            send_sem=fwd_send.at[i],
            recv_sem=cache_recv.at[there, core],
            device_id=(h_me, sibling),
            device_id_type=MESH,
        )
        copy.start()
        forwards.append(copy)

    row = lax.broadcasted_iota(jnp.int32, (rows, 1), 0)
    token = lax.rem(row, all_tokens)
    token = (lax.div(token, tokens) * n_ctx + c_me) * tokens + lax.rem(token, tokens)
    query_pos = token + offset_ref[0]
    lane = lax.broadcasted_iota(jnp.int32, (rows, 2 * span), 1)

    def score_step(i, top):
        at = chip_peer(i)
        arrival(cache_recv.at[at, 1 - core], piece(at, 1 - core)).wait_recv()
        s = (
            lax.dot_general(
                q_all[...],
                cache[at],
                (((1,), (1,)), ((), ())),
                preferred_element_type=jnp.float32,
            )
            * score_scale
        )
        s = jnp.where(lane + at * (2 * span) <= query_pos, s, -jnp.inf)
        scores[at] = s
        return jnp.maximum(top, jnp.max(s, axis=1, keepdims=True))

    unroll = chips if chips <= 4 else 1
    top = lax.fori_loop(
        0, chips, score_step, jnp.full((rows, 1), -jnp.inf, jnp.float32), unroll=unroll
    )
    acc[...] = jnp.zeros_like(acc)

    def value_step(i, total):
        at = chip_peer(i)
        expo = jnp.exp(scores[at] - top)
        acc[...] += jnp.dot(
            expo.astype(jnp.bfloat16), cache[at, :, :LATENT], preferred_element_type=jnp.float32
        )
        return total + jnp.sum(expo, axis=1, keepdims=True)

    total = lax.fori_loop(
        0, chips, value_step, jnp.zeros((rows, 1), jnp.float32), unroll=unroll
    )
    attended = (acc[...] / total).astype(jnp.bfloat16)
    load_uv.wait()
    for h in range(heads):
        heads_out[:, h * VDIM : (h + 1) * VDIM] = jnp.dot(
            attended[h * all_tokens : (h + 1) * all_tokens],
            uv[h],
            preferred_element_type=jnp.float32,
        )
    for p in range(n_head):
        slabs[p] = heads_out[p * tokens : (p + 1) * tokens, :].astype(jnp.bfloat16)

    mine = pl.ds(pl.multiple_of(h_me * o_cols, 128), o_cols)
    out_copies = []
    for i in range(1, n_head):
        there = head_peer(i)
        copy = pltpu.make_async_remote_copy(
            src_ref=slabs.at[there],
            dst_ref=out_ref.at[:, mine],
            send_sem=o_send.at[i],
            recv_sem=o_recv.at[h_me],
            device_id=(there, c_me),
            device_id_type=MESH,
        )
        copy.start()
        out_copies.append(copy)
    own_out = pltpu.make_async_copy(slabs.at[h_me], out_ref.at[:, mine], local_sem.at[5])
    own_out.start()

    for copy in cache_far + q_copies + [to_sibling] + forwards:
        copy.wait_send()
    own_out.wait()
    for i in range(1, n_head):
        there = head_peer(i)
        cols = pl.ds(pl.multiple_of(there * o_cols, 128), o_cols)
        arrival(o_recv.at[there], out_ref.at[:, cols]).wait_recv()
    for copy in out_copies:
        copy.wait_send()


def local(n_head, n_ctx, queries, w_uk, w_uv, latent_cache, span_offset):
    tokens = queries.shape[0]
    heads = w_uk.shape[0]
    span = latent_cache.shape[0]
    chips = n_ctx // 2
    all_tokens = n_head * tokens
    rows = heads * all_tokens
    bf16, f32 = jnp.bfloat16, jnp.float32
    dma = pltpu.SemaphoreType.DMA
    anywhere = pl.BlockSpec(memory_space=pl.ANY)
    return pl.pallas_call(
        functools.partial(kernel, n_head, n_ctx),
        out_shape=jax.ShapeDtypeStruct((tokens, n_head * heads * VDIM), bf16),
        in_specs=[anywhere] * 4 + [pl.BlockSpec(memory_space=pltpu.SMEM)],
        out_specs=pl.BlockSpec(memory_space=pltpu.VMEM),
        scratch_shapes=[
            pltpu.VMEM(queries.shape, bf16),
            pltpu.VMEM((n_head, tokens, heads * WIDTH), bf16),
            pltpu.VMEM((all_tokens, heads * WIDTH), f32),
            pltpu.VMEM(w_uk.shape, bf16),
            pltpu.VMEM(w_uv.shape, bf16),
            pltpu.VMEM((rows, LATENT + ROPE), bf16),
            pltpu.VMEM((chips, 2 * span, LATENT + ROPE), bf16),
            pltpu.VMEM((chips, rows, 2 * span), f32),
            pltpu.VMEM((rows, LATENT), f32),
            pltpu.VMEM((all_tokens, heads * VDIM), f32),
            pltpu.VMEM((n_head, tokens, heads * VDIM), bf16),
            dma((6,)),
            dma((n_head,)),
            dma((n_head,)),
            dma((chips,)),
            dma((chips,)),
            dma((chips, 2)),
            dma((n_head,)),
            dma((n_head,)),
        ],
        compiler_params=pltpu.CompilerParams(
            collective_id=0, has_side_effects=True, vmem_limit_bytes=40 * 1024 * 1024
        ),
    )(queries, w_uk, w_uv, latent_cache, span_offset)


def solution(mesh):
    return jax.shard_map(
        functools.partial(local, mesh.shape["head"], mesh.shape["ctx"]),
        mesh=mesh,
        in_specs=(
            P(("head", "ctx"), None),
            P("head", None, None),
            P("head", None, None),
            P("ctx", None),
            P(),
        ),
        out_specs=P(("head", "ctx"), None),
        check_vma=False,
    )
```

```python
import functools
import math

import jax
import jax.numpy as jnp
from jax import lax
from jax.experimental import pallas as pl
from jax.experimental.pallas import tpu as pltpu
from jax.sharding import PartitionSpec as P

NOPE = 128
ROPE = 64
LATENT = 512
VDIM = 128
WIDTH = NOPE + ROPE
MESH = pl.DeviceIdType.MESH

yarn_mscale = 0.1 * math.log(40.0) + 1.0
score_scale = WIDTH ** (-0.5) * yarn_mscale**2


def kernel(
    n_head, n_ctx, q_hbm, uk_hbm, uv_hbm, cache_hbm, offset_ref, out_ref,
    q_in, q_got, q_rows, uk, uv, q_all, cache, scores, acc, heads_out, slabs,
    local_sem, q_send, q_recv, own_send, fwd_send, cache_recv, o_send, o_recv,
):
    tokens = q_hbm.shape[0]
    heads = uk_hbm.shape[0]
    span = cache_hbm.shape[1]
    chips = n_ctx // 2
    all_tokens = n_head * tokens
    rows = heads * all_tokens
    q_cols = heads * WIDTH
    o_cols = heads * VDIM
    h_me = lax.axis_index("head")
    c_me = lax.axis_index("ctx")
    chip = c_me // 2
    core = c_me % 2
    sibling = chip * 2 + 1 - core

    def head_peer(i):
        return lax.rem(h_me + i, n_head)

    def chip_peer(i):
        return lax.rem(chip + i, chips)

    def piece(chip_at, core_at):
        return cache.at[chip_at, core_at]

    load_q = pltpu.make_async_copy(q_hbm, q_in, local_sem.at[0])
    load_cache = pltpu.make_async_copy(cache_hbm, piece(chip, core), local_sem.at[1])
    load_uk = pltpu.make_async_copy(uk_hbm, uk, local_sem.at[2])
    load_uv = pltpu.make_async_copy(uv_hbm, uv, local_sem.at[3])
    load_q.start()
    load_cache.start()
    load_uk.start()
    load_uv.start()

    barrier = pltpu.get_barrier_semaphore()
    for i in range(1, n_head):
        pl.semaphore_signal(barrier, inc=1, device_id=(head_peer(i), c_me), device_id_type=MESH)
    for i in range(1, chips):
        pl.semaphore_signal(
            barrier, inc=1, device_id=(h_me, chip_peer(i) * 2 + core), device_id_type=MESH
        )
    pl.semaphore_signal(barrier, inc=1, device_id=(h_me, sibling), device_id_type=MESH)
    load_q.wait()
    load_cache.wait()
    pl.semaphore_wait(barrier, n_head - 1 + chips)

    cache_far = []
    for i in range(1, chips):
        there = chip_peer(i)
        copy = pltpu.make_async_remote_copy(
            src_ref=piece(chip, core),
            dst_ref=piece(chip, core),
            send_sem=own_send.at[i],
            recv_sem=cache_recv.at[chip, core],
            device_id=(h_me, there * 2 + core),
            device_id_type=MESH,
        )
        copy.start()
        cache_far.append(copy)
    q_copies = []
    for i in range(1, n_head):
        there = head_peer(i)
        copy = pltpu.make_async_remote_copy(
            src_ref=q_in.at[:, pl.ds(pl.multiple_of(there * q_cols, 128), q_cols)],
            dst_ref=q_got.at[h_me],
            send_sem=q_send.at[i],
            recv_sem=q_recv.at[h_me],
            device_id=(there, c_me),
            device_id_type=MESH,
        )
        copy.start()
        q_copies.append(copy)
    to_sibling = pltpu.make_async_remote_copy(
        src_ref=piece(chip, core),
        dst_ref=piece(chip, core),
        send_sem=own_send.at[0],
        recv_sem=cache_recv.at[chip, core],
        device_id=(h_me, sibling),
        device_id_type=MESH,
    )
    to_sibling.start()
    own_q = pltpu.make_async_copy(
        q_in.at[:, pl.ds(pl.multiple_of(h_me * q_cols, 128), q_cols)],
        q_got.at[h_me],
        local_sem.at[4],
    )
    own_q.start()
    own_q.wait()

    def arrival(sem, dst, src=None):
        return pltpu.make_async_remote_copy(
            src_ref=dst,
            dst_ref=dst,
            send_sem=sem,
            recv_sem=sem,
            device_id=(h_me, sibling),
            device_id_type=MESH,
        )

    for i in range(1, n_head):
        there = head_peer(i)
        arrival(q_recv.at[there], q_got.at[there]).wait_recv()
    for p in range(n_head):
        q_rows[p * tokens : (p + 1) * tokens, :] = q_got[p].astype(jnp.float32)
    load_uk.wait()
    for pair in range(heads // 2):
        both = q_rows[:, pair * 2 * WIDTH : (pair + 1) * 2 * WIDTH].astype(jnp.bfloat16)
        for k in range(2):
            h = pair * 2 + k
            at = pl.ds(h * all_tokens, all_tokens)
            plain = both[:, k * WIDTH : k * WIDTH + NOPE]
            turned = both[:, k * WIDTH + NOPE : (k + 1) * WIDTH]
            q_all[at, :LATENT] = jnp.dot(
                plain, uk[h], preferred_element_type=jnp.float32
            ).astype(jnp.bfloat16)
            q_all[at, LATENT:] = turned

    forwards = []
    for i in range(1, chips):
        there = chip_peer(i)
        arrival(cache_recv.at[there, core], piece(there, core)).wait_recv()
        copy = pltpu.make_async_remote_copy(
            src_ref=piece(there, core),
            dst_ref=piece(there, core),
            send_sem=fwd_send.at[i],
            recv_sem=cache_recv.at[there, core],
            device_id=(h_me, sibling),
            device_id_type=MESH,
        )
        copy.start()
        forwards.append(copy)

    row = lax.broadcasted_iota(jnp.int32, (rows, 1), 0)
    token = lax.rem(row, all_tokens)
    token = (lax.div(token, tokens) * n_ctx + c_me) * tokens + lax.rem(token, tokens)
    query_pos = token + offset_ref[0]
    lane = lax.broadcasted_iota(jnp.int32, (rows, 2 * span), 1)

    def score_step(i, top):
        at = chip_peer(i)
        arrival(cache_recv.at[at, 1 - core], piece(at, 1 - core)).wait_recv()
        keys = jnp.concatenate([cache[at, 0], cache[at, 1]], axis=1)
        s = jnp.dot(q_all[...], keys, preferred_element_type=jnp.float32) * score_scale
        s = jnp.where(lane + at * (2 * span) <= query_pos, s, -jnp.inf)
        scores[at] = s
        return jnp.maximum(top, jnp.max(s, axis=1, keepdims=True))

    unroll = chips if chips <= 4 else 1
    top = lax.fori_loop(
        0, chips, score_step, jnp.full((rows, 1), -jnp.inf, jnp.float32), unroll=unroll
    )
    acc[...] = jnp.zeros_like(acc)

    def value_step(i, total):
        at = chip_peer(i)
        expo = jnp.exp(scores[at] - top)
        values = jnp.concatenate([cache[at, 0, :LATENT], cache[at, 1, :LATENT]], axis=1)
        acc[...] += lax.dot_general(
            expo.astype(jnp.bfloat16),
            values,
            (((1,), (1,)), ((), ())),
            preferred_element_type=jnp.float32,
        )
        return total + jnp.sum(expo, axis=1, keepdims=True)

    total = lax.fori_loop(
        0, chips, value_step, jnp.zeros((rows, 1), jnp.float32), unroll=unroll
    )
    attended = (acc[...] / total).astype(jnp.bfloat16)
    load_uv.wait()
    for h in range(heads):
        heads_out[:, h * VDIM : (h + 1) * VDIM] = jnp.dot(
            attended[h * all_tokens : (h + 1) * all_tokens],
            uv[h],
            preferred_element_type=jnp.float32,
        )
    for p in range(n_head):
        slabs[p] = heads_out[p * tokens : (p + 1) * tokens, :].astype(jnp.bfloat16)

    mine = pl.ds(pl.multiple_of(h_me * o_cols, 128), o_cols)
    out_copies = []
    for i in range(1, n_head):
        there = head_peer(i)
        copy = pltpu.make_async_remote_copy(
            src_ref=slabs.at[there],
            dst_ref=out_ref.at[:, mine],
            send_sem=o_send.at[i],
            recv_sem=o_recv.at[h_me],
            device_id=(there, c_me),
            device_id_type=MESH,
        )
        copy.start()
        out_copies.append(copy)
    own_out = pltpu.make_async_copy(slabs.at[h_me], out_ref.at[:, mine], local_sem.at[5])
    own_out.start()

    for copy in cache_far + q_copies + [to_sibling] + forwards:
        copy.wait_send()
    own_out.wait()
    for i in range(1, n_head):
        there = head_peer(i)
        cols = pl.ds(pl.multiple_of(there * o_cols, 128), o_cols)
        arrival(o_recv.at[there], out_ref.at[:, cols]).wait_recv()
    for copy in out_copies:
        copy.wait_send()


def local(n_head, n_ctx, queries, w_uk, w_uv, latent_cache, span_offset):
    tokens = queries.shape[0]
    heads = w_uk.shape[0]
    span = latent_cache.shape[0]
    chips = n_ctx // 2
    all_tokens = n_head * tokens
    rows = heads * all_tokens
    bf16, f32 = jnp.bfloat16, jnp.float32
    dma = pltpu.SemaphoreType.DMA
    anywhere = pl.BlockSpec(memory_space=pltpu.HBM)
    return pl.pallas_call(
        functools.partial(kernel, n_head, n_ctx),
        out_shape=jax.ShapeDtypeStruct((tokens, n_head * heads * VDIM), bf16),
        in_specs=[anywhere] * 4 + [pl.BlockSpec(memory_space=pltpu.SMEM)],
        out_specs=pl.BlockSpec(memory_space=pltpu.VMEM),
        scratch_shapes=[
            pltpu.VMEM(queries.shape, bf16),
            pltpu.VMEM((n_head, tokens, heads * WIDTH), bf16),
            pltpu.VMEM((all_tokens, heads * WIDTH), f32),
            pltpu.VMEM(w_uk.shape, bf16),
            pltpu.VMEM(w_uv.shape, bf16),
            pltpu.VMEM((rows, LATENT + ROPE), bf16),
            pltpu.VMEM((chips, 2, LATENT + ROPE, span), bf16),
            pltpu.VMEM((chips, rows, 2 * span), f32),
            pltpu.VMEM((rows, LATENT), f32),
            pltpu.VMEM((all_tokens, heads * VDIM), f32),
            pltpu.VMEM((n_head, tokens, heads * VDIM), bf16),
            dma((6,)),
            dma((n_head,)),
            dma((n_head,)),
            dma((chips,)),
            dma((chips,)),
            dma((chips, 2)),
            dma((n_head,)),
            dma((n_head,)),
        ],
        compiler_params=pltpu.CompilerParams(
            collective_id=0, has_side_effects=True, vmem_limit_bytes=64 * 1024 * 1024 - 64 * 1024
        ),
    )(queries, w_uk, w_uv, latent_cache.T, span_offset)


def solution(mesh):
    return jax.shard_map(
        functools.partial(local, mesh.shape["head"], mesh.shape["ctx"]),
        mesh=mesh,
        in_specs=(
            P(("head", "ctx"), None),
            P("head", None, None),
            P("head", None, None),
            P("ctx", None),
            P(),
        ),
        out_specs=P(("head", "ctx"), None),
        check_vma=False,
    )
```

```python
import functools
import math

import jax
import jax.numpy as jnp
from jax import lax
from jax.experimental import pallas as pl
from jax.experimental.pallas import tpu as pltpu
from jax.sharding import PartitionSpec as P

NOPE = 128
ROPE = 64
LATENT = 512
VDIM = 128
WIDTH = NOPE + ROPE
MESH = pl.DeviceIdType.MESH

yarn_mscale = 0.1 * math.log(40.0) + 1.0
score_scale = WIDTH ** (-0.5) * yarn_mscale**2


def kernel(
    n_head, n_ctx, q_hbm, uk_hbm, uv_hbm, cache_hbm, offset_ref, out_ref,
    q_in, q_got, q_rows, uk, uv, q_all, cache, scores, acc, heads_out, slabs,
    local_sem, q_send, q_recv, own_send, fwd_send, cache_recv, o_send, o_recv,
):
    tokens = q_hbm.shape[0]
    heads = uk_hbm.shape[0]
    span = cache_hbm.shape[1]
    chips = n_ctx // 2
    all_tokens = n_head * tokens
    rows = heads * all_tokens
    q_cols = heads * WIDTH
    o_cols = heads * VDIM
    h_me = lax.axis_index("head")
    c_me = lax.axis_index("ctx")
    chip = c_me // 2
    core = c_me % 2
    sibling = chip * 2 + 1 - core

    def head_peer(i):
        return lax.rem(h_me + i, n_head)

    def chip_peer(i):
        return lax.rem(chip + i, chips)

    def piece(chip_at, core_at):
        return cache.at[chip_at, core_at]

    load_q = pltpu.make_async_copy(q_hbm, q_in, local_sem.at[0])
    load_cache = pltpu.make_async_copy(cache_hbm, piece(chip, core), local_sem.at[1])
    load_uk = pltpu.make_async_copy(uk_hbm, uk, local_sem.at[2])
    load_uv = pltpu.make_async_copy(uv_hbm, uv, local_sem.at[3])
    load_q.start()
    load_cache.start()
    load_uk.start()
    load_uv.start()

    barrier = pltpu.get_barrier_semaphore()
    for i in range(1, n_head):
        pl.semaphore_signal(barrier, inc=1, device_id=(head_peer(i), c_me), device_id_type=MESH)
    for i in range(1, chips):
        pl.semaphore_signal(
            barrier, inc=1, device_id=(h_me, chip_peer(i) * 2 + core), device_id_type=MESH
        )
    pl.semaphore_signal(barrier, inc=1, device_id=(h_me, sibling), device_id_type=MESH)
    load_q.wait()
    load_cache.wait()
    pl.semaphore_wait(barrier, n_head - 1 + chips)

    cache_far = []
    for i in range(1, chips):
        there = chip_peer(i)
        copy = pltpu.make_async_remote_copy(
            src_ref=piece(chip, core),
            dst_ref=piece(chip, core),
            send_sem=own_send.at[i],
            recv_sem=cache_recv.at[chip, core],
            device_id=(h_me, there * 2 + core),
            device_id_type=MESH,
        )
        copy.start()
        cache_far.append(copy)
    q_copies = []
    for i in range(1, n_head):
        there = head_peer(i)
        copy = pltpu.make_async_remote_copy(
            src_ref=q_in.at[:, pl.ds(pl.multiple_of(there * q_cols, 128), q_cols)],
            dst_ref=q_got.at[h_me],
            send_sem=q_send.at[i],
            recv_sem=q_recv.at[h_me],
            device_id=(there, c_me),
            device_id_type=MESH,
        )
        copy.start()
        q_copies.append(copy)
    to_sibling = pltpu.make_async_remote_copy(
        src_ref=piece(chip, core),
        dst_ref=piece(chip, core),
        send_sem=own_send.at[0],
        recv_sem=cache_recv.at[chip, core],
        device_id=(h_me, sibling),
        device_id_type=MESH,
    )
    to_sibling.start()
    own_q = pltpu.make_async_copy(
        q_in.at[:, pl.ds(pl.multiple_of(h_me * q_cols, 128), q_cols)],
        q_got.at[h_me],
        local_sem.at[4],
    )
    own_q.start()
    own_q.wait()

    def arrival(sem, dst, src=None):
        return pltpu.make_async_remote_copy(
            src_ref=dst,
            dst_ref=dst,
            send_sem=sem,
            recv_sem=sem,
            device_id=(h_me, sibling),
            device_id_type=MESH,
        )

    for i in range(1, n_head):
        there = head_peer(i)
        arrival(q_recv.at[there], q_got.at[there]).wait_recv()
    for p in range(n_head):
        q_rows[p * tokens : (p + 1) * tokens, :] = q_got[p].astype(jnp.float32)
    load_uk.wait()
    for pair in range(heads // 2):
        both = q_rows[:, pair * 2 * WIDTH : (pair + 1) * 2 * WIDTH].astype(jnp.bfloat16)
        for k in range(2):
            h = pair * 2 + k
            at = pl.ds(h * all_tokens, all_tokens)
            plain = both[:, k * WIDTH : k * WIDTH + NOPE]
            turned = both[:, k * WIDTH + NOPE : (k + 1) * WIDTH]
            q_all[at, :LATENT] = jnp.dot(
                plain, uk[h], preferred_element_type=jnp.float32
            ).astype(jnp.bfloat16)
            q_all[at, LATENT:] = turned

    forwards = []
    for i in range(1, chips):
        there = chip_peer(i)
        arrival(cache_recv.at[there, core], piece(there, core)).wait_recv()
        copy = pltpu.make_async_remote_copy(
            src_ref=piece(there, core),
            dst_ref=piece(there, core),
            send_sem=fwd_send.at[i],
            recv_sem=cache_recv.at[there, core],
            device_id=(h_me, sibling),
            device_id_type=MESH,
        )
        copy.start()
        forwards.append(copy)

    parts = slabs.shape[0]
    row = lax.broadcasted_iota(jnp.int32, (rows // parts, 1), 0)
    token = lax.rem(row, all_tokens)
    token = (lax.div(token, tokens) * n_ctx + c_me) * tokens + lax.rem(token, tokens)
    query_pos = token + offset_ref[0]
    lane = lax.broadcasted_iota(jnp.int32, (rows // parts, 2 * span), 1)

    for i in range(chips):
        at = chip_peer(i)
        arrival(cache_recv.at[at, 1 - core], piece(at, 1 - core)).wait_recv()

    unroll = chips if chips <= 4 else 1
    part_heads = heads // parts
    part_rows = rows // parts
    part_cols = part_heads * VDIM
    out_copies = []
    own_outs = []
    for part in range(parts):
        here = slice(part * part_rows, (part + 1) * part_rows)

        def score_step(i, top):
            at = chip_peer(i)
            keys = jnp.concatenate([cache[at, 0], cache[at, 1]], axis=1)
            s = jnp.dot(q_all[here], keys, preferred_element_type=jnp.float32) * score_scale
            s = jnp.where(lane + at * (2 * span) <= query_pos, s, -jnp.inf)
            scores[at, here] = s
            return jnp.maximum(top, jnp.max(s, axis=1, keepdims=True))

        top = lax.fori_loop(
            0, chips, score_step, jnp.full((part_rows, 1), -jnp.inf, jnp.float32), unroll=unroll
        )
        acc[here] = jnp.zeros((part_rows, LATENT), jnp.float32)

        def value_step(i, total):
            at = chip_peer(i)
            expo = jnp.exp(scores[at, here] - top)
            values = jnp.concatenate([cache[at, 0, :LATENT], cache[at, 1, :LATENT]], axis=1)
            acc[here] += lax.dot_general(
                expo.astype(jnp.bfloat16),
                values,
                (((1,), (1,)), ((), ())),
                preferred_element_type=jnp.float32,
            )
            return total + jnp.sum(expo, axis=1, keepdims=True)

        total = lax.fori_loop(
            0, chips, value_step, jnp.zeros((part_rows, 1), jnp.float32), unroll=unroll
        )
        attended = (acc[here] / total).astype(jnp.bfloat16)
        if part == 0:
            load_uv.wait()
        for k in range(part_heads):
            h = part * part_heads + k
            heads_out[:, h * VDIM : (h + 1) * VDIM] = jnp.dot(
                attended[k * all_tokens : (k + 1) * all_tokens],
                uv[h],
                preferred_element_type=jnp.float32,
            )
        cols = slice(part * part_cols, (part + 1) * part_cols)
        for p in range(n_head):
            slabs[part, p] = heads_out[p * tokens : (p + 1) * tokens, cols].astype(jnp.bfloat16)
        start = pl.multiple_of(h_me * o_cols + part * part_cols, 128)
        mine = pl.ds(start, part_cols)
        for i in range(1, n_head):
            there = head_peer(i)
            copy = pltpu.make_async_remote_copy(
                src_ref=slabs.at[part, there],
                dst_ref=out_ref.at[:, mine],
                send_sem=o_send.at[part, i],
                recv_sem=o_recv.at[part, h_me],
                device_id=(there, c_me),
                device_id_type=MESH,
            )
            copy.start()
            out_copies.append(copy)
        own_out = pltpu.make_async_copy(
            slabs.at[part, h_me], out_ref.at[:, mine], local_sem.at[5 + part]
        )
        own_out.start()
        own_outs.append(own_out)

    for copy in cache_far + q_copies + [to_sibling] + forwards:
        copy.wait_send()
    for own_out in own_outs:
        own_out.wait()
    for part in range(parts):
        for i in range(1, n_head):
            there = head_peer(i)
            start = pl.multiple_of(there * o_cols + part * part_cols, 128)
            arrival(o_recv.at[part, there], out_ref.at[:, pl.ds(start, part_cols)]).wait_recv()
    for copy in out_copies:
        copy.wait_send()


def local(n_head, n_ctx, queries, w_uk, w_uv, latent_cache, span_offset):
    tokens = queries.shape[0]
    heads = w_uk.shape[0]
    span = latent_cache.shape[0]
    chips = n_ctx // 2
    all_tokens = n_head * tokens
    rows = heads * all_tokens
    parts = 2 if heads % 2 == 0 else 1
    bf16, f32 = jnp.bfloat16, jnp.float32
    dma = pltpu.SemaphoreType.DMA
    anywhere = pl.BlockSpec(memory_space=pltpu.HBM)
    return pl.pallas_call(
        functools.partial(kernel, n_head, n_ctx),
        out_shape=jax.ShapeDtypeStruct((tokens, n_head * heads * VDIM), bf16),
        in_specs=[anywhere] * 4 + [pl.BlockSpec(memory_space=pltpu.SMEM)],
        out_specs=pl.BlockSpec(memory_space=pltpu.VMEM),
        scratch_shapes=[
            pltpu.VMEM(queries.shape, bf16),
            pltpu.VMEM((n_head, tokens, heads * WIDTH), bf16),
            pltpu.VMEM((all_tokens, heads * WIDTH), f32),
            pltpu.VMEM(w_uk.shape, bf16),
            pltpu.VMEM(w_uv.shape, bf16),
            pltpu.VMEM((rows, LATENT + ROPE), bf16),
            pltpu.VMEM((chips, 2, LATENT + ROPE, span), bf16),
            pltpu.VMEM((chips, rows, 2 * span), f32),
            pltpu.VMEM((rows, LATENT), f32),
            pltpu.VMEM((all_tokens, heads * VDIM), f32),
            pltpu.VMEM((parts, n_head, tokens, heads // parts * VDIM), bf16),
            dma((5 + parts,)),
            dma((n_head,)),
            dma((n_head,)),
            dma((chips,)),
            dma((chips,)),
            dma((chips, 2)),
            dma((parts, n_head)),
            dma((parts, n_head)),
        ],
        compiler_params=pltpu.CompilerParams(
            collective_id=0, has_side_effects=True, vmem_limit_bytes=64 * 1024 * 1024 - 64 * 1024
        ),
    )(queries, w_uk, w_uv, latent_cache.T, span_offset)


def solution(mesh):
    return jax.shard_map(
        functools.partial(local, mesh.shape["head"], mesh.shape["ctx"]),
        mesh=mesh,
        in_specs=(
            P(("head", "ctx"), None),
            P("head", None, None),
            P("head", None, None),
            P("ctx", None),
            P(),
        ),
        out_specs=P(("head", "ctx"), None),
        check_vma=False,
    )
```

```python
import functools
import math

import jax
import jax.numpy as jnp
from jax import lax
from jax.experimental import pallas as pl
from jax.experimental.pallas import tpu as pltpu
from jax.sharding import PartitionSpec as P

NOPE = 128
ROPE = 64
LATENT = 512
VDIM = 128
WIDTH = NOPE + ROPE
MESH = pl.DeviceIdType.MESH

yarn_mscale = 0.1 * math.log(40.0) + 1.0
score_scale = WIDTH ** (-0.5) * yarn_mscale**2


def kernel(
    n_head, n_ctx, q_hbm, uk_hbm, uv_hbm, cache_hbm, offset_ref, out_ref,
    q_in, q_got, q_rows, uk, uv, q_all, cache, scores, acc, heads_out, slabs,
    local_sem, q_send, q_recv, own_send, fwd_send, cache_recv, o_send, o_recv,
):
    tokens = q_hbm.shape[0]
    heads = uk_hbm.shape[0]
    span = cache_hbm.shape[1]
    chips = n_ctx // 2
    all_tokens = n_head * tokens
    rows = heads * all_tokens
    q_cols = heads * WIDTH
    o_cols = heads * VDIM
    h_me = lax.axis_index("head")
    c_me = lax.axis_index("ctx")
    chip = c_me // 2
    core = c_me % 2
    sibling = chip * 2 + 1 - core

    def head_peer(i):
        return lax.rem(h_me + i, n_head)

    def chip_peer(i):
        return lax.rem(chip + i, chips)

    def piece(chip_at, core_at):
        return cache.at[chip_at, core_at]

    load_q = pltpu.make_async_copy(q_hbm, q_in, local_sem.at[0])
    load_cache = pltpu.make_async_copy(cache_hbm, piece(chip, core), local_sem.at[1])
    load_uk = pltpu.make_async_copy(uk_hbm, uk, local_sem.at[2])
    load_uv = pltpu.make_async_copy(uv_hbm, uv, local_sem.at[3])
    load_q.start()
    load_cache.start()
    load_uk.start()
    load_uv.start()

    barrier = pltpu.get_barrier_semaphore()
    for i in range(1, n_head):
        pl.semaphore_signal(barrier, inc=1, device_id=(head_peer(i), c_me), device_id_type=MESH)
    for i in range(1, chips):
        pl.semaphore_signal(
            barrier, inc=1, device_id=(h_me, chip_peer(i) * 2 + core), device_id_type=MESH
        )
    pl.semaphore_signal(barrier, inc=1, device_id=(h_me, sibling), device_id_type=MESH)
    load_q.wait()
    load_cache.wait()
    pl.semaphore_wait(barrier, n_head - 1 + chips)

    cache_far = []
    for i in range(1, chips):
        there = chip_peer(i)
        copy = pltpu.make_async_remote_copy(
            src_ref=piece(chip, core),
            dst_ref=piece(chip, core),
            send_sem=own_send.at[i],
            recv_sem=cache_recv.at[chip, core],
            device_id=(h_me, there * 2 + core),
            device_id_type=MESH,
        )
        copy.start()
        cache_far.append(copy)
    q_copies = []
    for i in range(1, n_head):
        there = head_peer(i)
        copy = pltpu.make_async_remote_copy(
            src_ref=q_in.at[:, pl.ds(pl.multiple_of(there * q_cols, 128), q_cols)],
            dst_ref=q_got.at[h_me],
            send_sem=q_send.at[i],
            recv_sem=q_recv.at[h_me],
            device_id=(there, c_me),
            device_id_type=MESH,
        )
        copy.start()
        q_copies.append(copy)
    to_sibling = pltpu.make_async_remote_copy(
        src_ref=piece(chip, core),
        dst_ref=piece(chip, core),
        send_sem=own_send.at[0],
        recv_sem=cache_recv.at[chip, core],
        device_id=(h_me, sibling),
        device_id_type=MESH,
    )
    to_sibling.start()
    own_q = pltpu.make_async_copy(
        q_in.at[:, pl.ds(pl.multiple_of(h_me * q_cols, 128), q_cols)],
        q_got.at[h_me],
        local_sem.at[4],
    )
    own_q.start()
    own_q.wait()

    def arrival(sem, dst, src=None):
        return pltpu.make_async_remote_copy(
            src_ref=dst,
            dst_ref=dst,
            send_sem=sem,
            recv_sem=sem,
            device_id=(h_me, sibling),
            device_id_type=MESH,
        )

    for i in range(1, n_head):
        there = head_peer(i)
        arrival(q_recv.at[there], q_got.at[there]).wait_recv()
    for p in range(n_head):
        q_rows[p * tokens : (p + 1) * tokens, :] = q_got[p].astype(jnp.float32)
    load_uk.wait()
    for pair in range(heads // 2):
        both = q_rows[:, pair * 2 * WIDTH : (pair + 1) * 2 * WIDTH].astype(jnp.bfloat16)
        for k in range(2):
            h = pair * 2 + k
            at = pl.ds(h * all_tokens, all_tokens)
            plain = both[:, k * WIDTH : k * WIDTH + NOPE]
            turned = both[:, k * WIDTH + NOPE : (k + 1) * WIDTH]
            q_all[at, :LATENT] = jnp.dot(
                plain, uk[h], preferred_element_type=jnp.float32
            ).astype(jnp.bfloat16)
            q_all[at, LATENT:] = turned

    forwards = []
    for i in range(1, chips):
        there = chip_peer(i)
        arrival(cache_recv.at[there, core], piece(there, core)).wait_recv()
        copy = pltpu.make_async_remote_copy(
            src_ref=piece(there, core),
            dst_ref=piece(there, core),
            send_sem=fwd_send.at[i],
            recv_sem=cache_recv.at[there, core],
            device_id=(h_me, sibling),
            device_id_type=MESH,
        )
        copy.start()
        forwards.append(copy)

    row = lax.broadcasted_iota(jnp.int32, (rows, 1), 0)
    token = lax.rem(row, all_tokens)
    token = (lax.div(token, tokens) * n_ctx + c_me) * tokens + lax.rem(token, tokens)
    query_pos = token + offset_ref[0]
    lane = lax.broadcasted_iota(jnp.int32, (rows, 2 * span), 1)

    def score_step(i, top):
        at = chip_peer(i)
        arrival(cache_recv.at[at, 1 - core], piece(at, 1 - core)).wait_recv()
        keys = jnp.concatenate([cache[at, 0], cache[at, 1]], axis=1)
        s = jnp.dot(q_all[...], keys, preferred_element_type=jnp.float32) * score_scale
        s = jnp.where(lane + at * (2 * span) <= query_pos, s, -jnp.inf)
        scores[at] = s
        return jnp.maximum(top, jnp.max(s, axis=1, keepdims=True))

    unroll = chips if chips <= 4 else 1
    top = lax.fori_loop(
        0, chips, score_step, jnp.full((rows, 1), -jnp.inf, jnp.float32), unroll=unroll
    )
    acc[...] = jnp.zeros_like(acc)

    def value_step(i, total):
        at = chip_peer(i)
        expo = jnp.exp(scores[at] - top)
        values = jnp.concatenate([cache[at, 0, :LATENT], cache[at, 1, :LATENT]], axis=1)
        acc[...] += lax.dot_general(
            expo.astype(jnp.bfloat16),
            values,
            (((1,), (1,)), ((), ())),
            preferred_element_type=jnp.float32,
        )
        return total + jnp.sum(expo, axis=1, keepdims=True)

    total = lax.fori_loop(
        0, chips, value_step, jnp.zeros((rows, 1), jnp.float32), unroll=unroll
    )
    attended = (acc[...] / total).astype(jnp.bfloat16)
    load_uv.wait()
    for h in range(heads):
        heads_out[:, h * VDIM : (h + 1) * VDIM] = jnp.dot(
            attended[h * all_tokens : (h + 1) * all_tokens],
            uv[h],
            preferred_element_type=jnp.float32,
        )
    for p in range(n_head):
        slabs[p] = heads_out[p * tokens : (p + 1) * tokens, :].astype(jnp.bfloat16)

    mine = pl.ds(pl.multiple_of(h_me * o_cols, 128), o_cols)
    out_copies = []
    for i in range(1, n_head):
        there = head_peer(i)
        copy = pltpu.make_async_remote_copy(
            src_ref=slabs.at[there],
            dst_ref=out_ref.at[:, mine],
            send_sem=o_send.at[i],
            recv_sem=o_recv.at[h_me],
            device_id=(there, c_me),
            device_id_type=MESH,
        )
        copy.start()
        out_copies.append(copy)
    own_out = pltpu.make_async_copy(slabs.at[h_me], out_ref.at[:, mine], local_sem.at[5])
    own_out.start()

    for copy in cache_far + q_copies + [to_sibling] + forwards:
        copy.wait_send()
    own_out.wait()
    for i in range(1, n_head):
        there = head_peer(i)
        cols = pl.ds(pl.multiple_of(there * o_cols, 128), o_cols)
        arrival(o_recv.at[there], out_ref.at[:, cols]).wait_recv()
    for copy in out_copies:
        copy.wait_send()


def local(n_head, n_ctx, queries, w_uk, w_uv, latent_cache, span_offset):
    tokens = queries.shape[0]
    heads = w_uk.shape[0]
    span = latent_cache.shape[0]
    chips = n_ctx // 2
    all_tokens = n_head * tokens
    rows = heads * all_tokens
    bf16, f32 = jnp.bfloat16, jnp.float32
    dma = pltpu.SemaphoreType.DMA
    anywhere = pl.BlockSpec(memory_space=pl.ANY)
    return pl.pallas_call(
        functools.partial(kernel, n_head, n_ctx),
        out_shape=jax.ShapeDtypeStruct((tokens, n_head * heads * VDIM), bf16),
        in_specs=[anywhere] * 4 + [pl.BlockSpec(memory_space=pltpu.SMEM)],
        out_specs=anywhere,
        scratch_shapes=[
            pltpu.VMEM(queries.shape, bf16),
            pltpu.VMEM((n_head, tokens, heads * WIDTH), bf16),
            pltpu.VMEM((all_tokens, heads * WIDTH), f32),
            pltpu.VMEM(w_uk.shape, bf16),
            pltpu.VMEM(w_uv.shape, bf16),
            pltpu.VMEM((rows, LATENT + ROPE), bf16),
            pltpu.VMEM((chips, 2, LATENT + ROPE, span), bf16),
            pltpu.VMEM((chips, rows, 2 * span), f32),
            pltpu.VMEM((rows, LATENT), f32),
            pltpu.VMEM((all_tokens, heads * VDIM), f32),
            pltpu.VMEM((n_head, tokens, heads * VDIM), bf16),
            dma((6,)),
            dma((n_head,)),
            dma((n_head,)),
            dma((chips,)),
            dma((chips,)),
            dma((chips, 2)),
            dma((n_head,)),
            dma((n_head,)),
        ],
        compiler_params=pltpu.CompilerParams(
            collective_id=0, has_side_effects=True, vmem_limit_bytes=64 * 1024 * 1024 - 64 * 1024
        ),
    )(queries, w_uk, w_uv, latent_cache.T, span_offset)


def solution(mesh):
    return jax.shard_map(
        functools.partial(local, mesh.shape["head"], mesh.shape["ctx"]),
        mesh=mesh,
        in_specs=(
            P(("head", "ctx"), None),
            P("head", None, None),
            P("head", None, None),
            P("ctx", None),
            P(),
        ),
        out_specs=P(("head", "ctx"), None),
        check_vma=False,
    )
```

```python
import functools
import math

import jax
import jax.numpy as jnp
from jax import lax
from jax.experimental import pallas as pl
from jax.experimental.pallas import tpu as pltpu
from jax.sharding import PartitionSpec as P

NOPE = 128
ROPE = 64
LATENT = 512
VDIM = 128
WIDTH = NOPE + ROPE
MESH = pl.DeviceIdType.MESH

yarn_mscale = 0.1 * math.log(40.0) + 1.0
score_scale = WIDTH ** (-0.5) * yarn_mscale**2


def kernel(
    n_head, n_ctx, q_hbm, uk_hbm, uv_hbm, cache_hbm, offset_ref, out_ref,
    q_in, q_got, q_rows, uk, uv, q_all, cache, scores, acc, heads_out, slabs,
    local_sem, q_send, q_recv, own_send, fwd_send, cache_recv, o_send, o_recv,
):
    tokens = q_hbm.shape[0]
    heads = uk_hbm.shape[0]
    span = cache_hbm.shape[1]
    chips = n_ctx // 2
    all_tokens = n_head * tokens
    rows = heads * all_tokens
    q_cols = heads * WIDTH
    o_cols = heads * VDIM
    h_me = lax.axis_index("head")
    c_me = lax.axis_index("ctx")
    chip = c_me // 2
    core = c_me % 2
    sibling = chip * 2 + 1 - core

    def head_peer(i):
        return lax.rem(h_me + i, n_head)

    def chip_peer(i):
        return lax.rem(chip + i, chips)

    def piece(chip_at, core_at):
        return cache.at[chip_at, core_at]

    load_q = pltpu.make_async_copy(q_hbm, q_in, local_sem.at[0])
    load_cache = pltpu.make_async_copy(cache_hbm, piece(chip, core), local_sem.at[1])
    load_uk = pltpu.make_async_copy(uk_hbm, uk, local_sem.at[2])
    load_uv = pltpu.make_async_copy(uv_hbm, uv, local_sem.at[3])
    load_q.start()
    load_cache.start()

    barrier = pltpu.get_barrier_semaphore()
    for i in range(1, n_head):
        pl.semaphore_signal(barrier, inc=1, device_id=(head_peer(i), c_me), device_id_type=MESH)
    for i in range(1, chips):
        pl.semaphore_signal(
            barrier, inc=1, device_id=(h_me, chip_peer(i) * 2 + core), device_id_type=MESH
        )
    pl.semaphore_signal(barrier, inc=1, device_id=(h_me, sibling), device_id_type=MESH)
    load_q.wait()
    load_uk.start()
    load_uv.start()
    pl.semaphore_wait(barrier, n_head - 1 + chips)

    q_copies = []
    for i in range(1, n_head):
        there = head_peer(i)
        copy = pltpu.make_async_remote_copy(
            src_ref=q_in.at[:, pl.ds(pl.multiple_of(there * q_cols, 128), q_cols)],
            dst_ref=q_got.at[h_me],
            send_sem=q_send.at[i],
            recv_sem=q_recv.at[h_me],
            device_id=(there, c_me),
            device_id_type=MESH,
        )
        copy.start()
        q_copies.append(copy)
    load_cache.wait()
    cache_far = []
    for i in range(1, chips):
        there = chip_peer(i)
        copy = pltpu.make_async_remote_copy(
            src_ref=piece(chip, core),
            dst_ref=piece(chip, core),
            send_sem=own_send.at[i],
            recv_sem=cache_recv.at[chip, core],
            device_id=(h_me, there * 2 + core),
            device_id_type=MESH,
        )
        copy.start()
        cache_far.append(copy)
    to_sibling = pltpu.make_async_remote_copy(
        src_ref=piece(chip, core),
        dst_ref=piece(chip, core),
        send_sem=own_send.at[0],
        recv_sem=cache_recv.at[chip, core],
        device_id=(h_me, sibling),
        device_id_type=MESH,
    )
    to_sibling.start()
    own_q = pltpu.make_async_copy(
        q_in.at[:, pl.ds(pl.multiple_of(h_me * q_cols, 128), q_cols)],
        q_got.at[h_me],
        local_sem.at[4],
    )
    own_q.start()
    own_q.wait()

    def arrival(sem, dst, src=None):
        return pltpu.make_async_remote_copy(
            src_ref=dst,
            dst_ref=dst,
            send_sem=sem,
            recv_sem=sem,
            device_id=(h_me, sibling),
            device_id_type=MESH,
        )

    for i in range(1, n_head):
        there = head_peer(i)
        arrival(q_recv.at[there], q_got.at[there]).wait_recv()
    for p in range(n_head):
        q_rows[p * tokens : (p + 1) * tokens, :] = q_got[p].astype(jnp.float32)
    load_uk.wait()
    for pair in range(heads // 2):
        both = q_rows[:, pair * 2 * WIDTH : (pair + 1) * 2 * WIDTH].astype(jnp.bfloat16)
        for k in range(2):
            h = pair * 2 + k
            at = pl.ds(h * all_tokens, all_tokens)
            plain = both[:, k * WIDTH : k * WIDTH + NOPE]
            turned = both[:, k * WIDTH + NOPE : (k + 1) * WIDTH]
            q_all[at, :LATENT] = jnp.dot(
                plain, uk[h], preferred_element_type=jnp.float32
            ).astype(jnp.bfloat16)
            q_all[at, LATENT:] = turned

    forwards = []
    for i in range(1, chips):
        there = chip_peer(i)
        arrival(cache_recv.at[there, core], piece(there, core)).wait_recv()
        copy = pltpu.make_async_remote_copy(
            src_ref=piece(there, core),
            dst_ref=piece(there, core),
            send_sem=fwd_send.at[i],
            recv_sem=cache_recv.at[there, core],
            device_id=(h_me, sibling),
            device_id_type=MESH,
        )
        copy.start()
        forwards.append(copy)

    row = lax.broadcasted_iota(jnp.int32, (rows, 1), 0)
    token = lax.rem(row, all_tokens)
    token = (lax.div(token, tokens) * n_ctx + c_me) * tokens + lax.rem(token, tokens)
    query_pos = token + offset_ref[0]
    lane = lax.broadcasted_iota(jnp.int32, (rows, 2 * span), 1)

    def score_step(i, top):
        at = chip_peer(i)
        arrival(cache_recv.at[at, 1 - core], piece(at, 1 - core)).wait_recv()
        keys = jnp.concatenate([cache[at, 0], cache[at, 1]], axis=1)
        s = jnp.dot(q_all[...], keys, preferred_element_type=jnp.float32) * score_scale
        s = jnp.where(lane + at * (2 * span) <= query_pos, s, -jnp.inf)
        scores[at] = s
        return jnp.maximum(top, jnp.max(s, axis=1, keepdims=True))

    unroll = chips if chips <= 4 else 1
    top = lax.fori_loop(
        0, chips, score_step, jnp.full((rows, 1), -jnp.inf, jnp.float32), unroll=unroll
    )
    acc[...] = jnp.zeros_like(acc)

    def value_step(i, total):
        at = chip_peer(i)
        expo = jnp.exp(scores[at] - top)
        values = jnp.concatenate([cache[at, 0, :LATENT], cache[at, 1, :LATENT]], axis=1)
        acc[...] += lax.dot_general(
            expo.astype(jnp.bfloat16),
            values,
            (((1,), (1,)), ((), ())),
            preferred_element_type=jnp.float32,
        )
        return total + jnp.sum(expo, axis=1, keepdims=True)

    total = lax.fori_loop(
        0, chips, value_step, jnp.zeros((rows, 1), jnp.float32), unroll=unroll
    )
    attended = (acc[...] / total).astype(jnp.bfloat16)
    load_uv.wait()
    for h in range(heads):
        heads_out[:, h * VDIM : (h + 1) * VDIM] = jnp.dot(
            attended[h * all_tokens : (h + 1) * all_tokens],
            uv[h],
            preferred_element_type=jnp.float32,
        )
    for p in range(n_head):
        slabs[p] = heads_out[p * tokens : (p + 1) * tokens, :].astype(jnp.bfloat16)

    mine = pl.ds(pl.multiple_of(h_me * o_cols, 128), o_cols)
    out_copies = []
    for i in range(1, n_head):
        there = head_peer(i)
        copy = pltpu.make_async_remote_copy(
            src_ref=slabs.at[there],
            dst_ref=out_ref.at[:, mine],
            send_sem=o_send.at[i],
            recv_sem=o_recv.at[h_me],
            device_id=(there, c_me),
            device_id_type=MESH,
        )
        copy.start()
        out_copies.append(copy)
    own_out = pltpu.make_async_copy(slabs.at[h_me], out_ref.at[:, mine], local_sem.at[5])
    own_out.start()

    for copy in cache_far + q_copies + [to_sibling] + forwards:
        copy.wait_send()
    own_out.wait()
    for i in range(1, n_head):
        there = head_peer(i)
        cols = pl.ds(pl.multiple_of(there * o_cols, 128), o_cols)
        arrival(o_recv.at[there], out_ref.at[:, cols]).wait_recv()
    for copy in out_copies:
        copy.wait_send()


def local(n_head, n_ctx, queries, w_uk, w_uv, latent_cache, span_offset):
    tokens = queries.shape[0]
    heads = w_uk.shape[0]
    span = latent_cache.shape[0]
    chips = n_ctx // 2
    all_tokens = n_head * tokens
    rows = heads * all_tokens
    bf16, f32 = jnp.bfloat16, jnp.float32
    dma = pltpu.SemaphoreType.DMA
    anywhere = pl.BlockSpec(memory_space=pl.ANY)
    return pl.pallas_call(
        functools.partial(kernel, n_head, n_ctx),
        out_shape=jax.ShapeDtypeStruct((tokens, n_head * heads * VDIM), bf16),
        in_specs=[anywhere] * 4 + [pl.BlockSpec(memory_space=pltpu.SMEM)],
        out_specs=anywhere,
        scratch_shapes=[
            pltpu.VMEM(queries.shape, bf16),
            pltpu.VMEM((n_head, tokens, heads * WIDTH), bf16),
            pltpu.VMEM((all_tokens, heads * WIDTH), f32),
            pltpu.VMEM(w_uk.shape, bf16),
            pltpu.VMEM(w_uv.shape, bf16),
            pltpu.VMEM((rows, LATENT + ROPE), bf16),
            pltpu.VMEM((chips, 2, LATENT + ROPE, span), bf16),
            pltpu.VMEM((chips, rows, 2 * span), f32),
            pltpu.VMEM((rows, LATENT), f32),
            pltpu.VMEM((all_tokens, heads * VDIM), f32),
            pltpu.VMEM((n_head, tokens, heads * VDIM), bf16),
            dma((6,)),
            dma((n_head,)),
            dma((n_head,)),
            dma((chips,)),
            dma((chips,)),
            dma((chips, 2)),
            dma((n_head,)),
            dma((n_head,)),
        ],
        compiler_params=pltpu.CompilerParams(
            collective_id=0, has_side_effects=True, vmem_limit_bytes=64 * 1024 * 1024 - 64 * 1024
        ),
    )(queries, w_uk, w_uv, latent_cache.T, span_offset)


def solution(mesh):
    return jax.shard_map(
        functools.partial(local, mesh.shape["head"], mesh.shape["ctx"]),
        mesh=mesh,
        in_specs=(
            P(("head", "ctx"), None),
            P("head", None, None),
            P("head", None, None),
            P("ctx", None),
            P(),
        ),
        out_specs=P(("head", "ctx"), None),
        check_vma=False,
    )
```

```python
import functools
import math

import jax
import jax.numpy as jnp
from jax import lax
from jax.experimental import pallas as pl
from jax.experimental.pallas import tpu as pltpu
from jax.sharding import PartitionSpec as P

NOPE = 128
ROPE = 64
LATENT = 512
VDIM = 128
WIDTH = NOPE + ROPE
MESH = pl.DeviceIdType.MESH

yarn_mscale = 0.1 * math.log(40.0) + 1.0
score_scale = WIDTH ** (-0.5) * yarn_mscale**2


def kernel(
    n_head, n_ctx, q_hbm, uk_hbm, uv_hbm, cache_hbm, offset_ref, out_ref,
    q_in, q_got, q_rows, uk, uv, q_all, cache, scores, acc, heads_out, slabs,
    local_sem, q_send, q_recv, own_send, fwd_send, cache_recv, o_send, o_recv,
):
    tokens = q_hbm.shape[0]
    heads = uk_hbm.shape[0]
    span = cache_hbm.shape[1]
    chips = n_ctx // 2
    all_tokens = n_head * tokens
    rows = heads * all_tokens
    q_cols = heads * WIDTH
    o_cols = heads * VDIM
    h_me = lax.axis_index("head")
    c_me = lax.axis_index("ctx")
    chip = c_me // 2
    core = c_me % 2
    sibling = chip * 2 + 1 - core

    far_first = sorted(range(1, n_head), key=lambda i: abs(2 * i - n_head))

    def head_peer(i):
        return lax.rem(h_me + i, n_head)

    def chip_peer(i):
        return lax.rem(chip + i, chips)

    def piece(chip_at, core_at):
        return cache.at[chip_at, core_at]

    load_q = pltpu.make_async_copy(q_hbm, q_in, local_sem.at[0])
    load_cache = pltpu.make_async_copy(cache_hbm, piece(chip, core), local_sem.at[1])
    load_uk = pltpu.make_async_copy(uk_hbm, uk, local_sem.at[2])
    load_uv = pltpu.make_async_copy(uv_hbm, uv, local_sem.at[3])
    load_q.start()
    load_cache.start()

    barrier = pltpu.get_barrier_semaphore()
    for i in range(1, n_head):
        pl.semaphore_signal(barrier, inc=1, device_id=(head_peer(i), c_me), device_id_type=MESH)
    for i in range(1, chips):
        pl.semaphore_signal(
            barrier, inc=1, device_id=(h_me, chip_peer(i) * 2 + core), device_id_type=MESH
        )
    pl.semaphore_signal(barrier, inc=1, device_id=(h_me, sibling), device_id_type=MESH)
    load_q.wait()
    load_uk.start()
    load_uv.start()
    pl.semaphore_wait(barrier, n_head - 1 + chips)

    q_copies = []
    for i in far_first:
        there = head_peer(i)
        copy = pltpu.make_async_remote_copy(
            src_ref=q_in.at[:, pl.ds(pl.multiple_of(there * q_cols, 128), q_cols)],
            dst_ref=q_got.at[h_me],
            send_sem=q_send.at[i],
            recv_sem=q_recv.at[h_me],
            device_id=(there, c_me),
            device_id_type=MESH,
        )
        copy.start()
        q_copies.append(copy)
    load_cache.wait()
    cache_far = []
    for i in range(1, chips):
        there = chip_peer(i)
        copy = pltpu.make_async_remote_copy(
            src_ref=piece(chip, core),
            dst_ref=piece(chip, core),
            send_sem=own_send.at[i],
            recv_sem=cache_recv.at[chip, core],
            device_id=(h_me, there * 2 + core),
            device_id_type=MESH,
        )
        copy.start()
        cache_far.append(copy)
    to_sibling = pltpu.make_async_remote_copy(
        src_ref=piece(chip, core),
        dst_ref=piece(chip, core),
        send_sem=own_send.at[0],
        recv_sem=cache_recv.at[chip, core],
        device_id=(h_me, sibling),
        device_id_type=MESH,
    )
    to_sibling.start()
    own_q = pltpu.make_async_copy(
        q_in.at[:, pl.ds(pl.multiple_of(h_me * q_cols, 128), q_cols)],
        q_got.at[h_me],
        local_sem.at[4],
    )
    own_q.start()
    own_q.wait()

    def arrival(sem, dst, src=None):
        return pltpu.make_async_remote_copy(
            src_ref=dst,
            dst_ref=dst,
            send_sem=sem,
            recv_sem=sem,
            device_id=(h_me, sibling),
            device_id_type=MESH,
        )

    for i in range(1, n_head):
        there = head_peer(i)
        arrival(q_recv.at[there], q_got.at[there]).wait_recv()
    for p in range(n_head):
        q_rows[p * tokens : (p + 1) * tokens, :] = q_got[p].astype(jnp.float32)
    load_uk.wait()
    for pair in range(heads // 2):
        both = q_rows[:, pair * 2 * WIDTH : (pair + 1) * 2 * WIDTH].astype(jnp.bfloat16)
        for k in range(2):
            h = pair * 2 + k
            at = pl.ds(h * all_tokens, all_tokens)
            plain = both[:, k * WIDTH : k * WIDTH + NOPE]
            turned = both[:, k * WIDTH + NOPE : (k + 1) * WIDTH]
            q_all[at, :LATENT] = jnp.dot(
                plain, uk[h], preferred_element_type=jnp.float32
            ).astype(jnp.bfloat16)
            q_all[at, LATENT:] = turned

    forwards = []
    for i in range(1, chips):
        there = chip_peer(i)
        arrival(cache_recv.at[there, core], piece(there, core)).wait_recv()
        copy = pltpu.make_async_remote_copy(
            src_ref=piece(there, core),
            dst_ref=piece(there, core),
            send_sem=fwd_send.at[i],
            recv_sem=cache_recv.at[there, core],
            device_id=(h_me, sibling),
            device_id_type=MESH,
        )
        copy.start()
        forwards.append(copy)

    row = lax.broadcasted_iota(jnp.int32, (rows, 1), 0)
    token = lax.rem(row, all_tokens)
    token = (lax.div(token, tokens) * n_ctx + c_me) * tokens + lax.rem(token, tokens)
    query_pos = token + offset_ref[0]
    lane = lax.broadcasted_iota(jnp.int32, (rows, 2 * span), 1)

    def score_step(i, top):
        at = chip_peer(i)
        arrival(cache_recv.at[at, 1 - core], piece(at, 1 - core)).wait_recv()
        keys = jnp.concatenate([cache[at, 0], cache[at, 1]], axis=1)
        s = jnp.dot(q_all[...], keys, preferred_element_type=jnp.float32) * score_scale
        s = jnp.where(lane + at * (2 * span) <= query_pos, s, -jnp.inf)
        scores[at] = s
        return jnp.maximum(top, jnp.max(s, axis=1, keepdims=True))

    unroll = chips if chips <= 4 else 1
    top = lax.fori_loop(
        0, chips, score_step, jnp.full((rows, 1), -jnp.inf, jnp.float32), unroll=unroll
    )
    acc[...] = jnp.zeros_like(acc)

    def value_step(i, total):
        at = chip_peer(i)
        expo = jnp.exp(scores[at] - top)
        values = jnp.concatenate([cache[at, 0, :LATENT], cache[at, 1, :LATENT]], axis=1)
        acc[...] += lax.dot_general(
            expo.astype(jnp.bfloat16),
            values,
            (((1,), (1,)), ((), ())),
            preferred_element_type=jnp.float32,
        )
        return total + jnp.sum(expo, axis=1, keepdims=True)

    total = lax.fori_loop(
        0, chips, value_step, jnp.zeros((rows, 1), jnp.float32), unroll=unroll
    )
    attended = (acc[...] / total).astype(jnp.bfloat16)
    load_uv.wait()
    for h in range(heads):
        heads_out[:, h * VDIM : (h + 1) * VDIM] = jnp.dot(
            attended[h * all_tokens : (h + 1) * all_tokens],
            uv[h],
            preferred_element_type=jnp.float32,
        )
    for p in range(n_head):
        slabs[p] = heads_out[p * tokens : (p + 1) * tokens, :].astype(jnp.bfloat16)

    mine = pl.ds(pl.multiple_of(h_me * o_cols, 128), o_cols)
    out_copies = []
    for i in far_first:
        there = head_peer(i)
        copy = pltpu.make_async_remote_copy(
            src_ref=slabs.at[there],
            dst_ref=out_ref.at[:, mine],
            send_sem=o_send.at[i],
            recv_sem=o_recv.at[h_me],
            device_id=(there, c_me),
            device_id_type=MESH,
        )
        copy.start()
        out_copies.append(copy)
    own_out = pltpu.make_async_copy(slabs.at[h_me], out_ref.at[:, mine], local_sem.at[5])
    own_out.start()

    for copy in cache_far + q_copies + [to_sibling] + forwards:
        copy.wait_send()
    own_out.wait()
    for i in range(1, n_head):
        there = head_peer(i)
        cols = pl.ds(pl.multiple_of(there * o_cols, 128), o_cols)
        arrival(o_recv.at[there], out_ref.at[:, cols]).wait_recv()
    for copy in out_copies:
        copy.wait_send()


def local(n_head, n_ctx, queries, w_uk, w_uv, latent_cache, span_offset):
    tokens = queries.shape[0]
    heads = w_uk.shape[0]
    span = latent_cache.shape[0]
    chips = n_ctx // 2
    all_tokens = n_head * tokens
    rows = heads * all_tokens
    bf16, f32 = jnp.bfloat16, jnp.float32
    dma = pltpu.SemaphoreType.DMA
    anywhere = pl.BlockSpec(memory_space=pl.ANY)
    return pl.pallas_call(
        functools.partial(kernel, n_head, n_ctx),
        out_shape=jax.ShapeDtypeStruct((tokens, n_head * heads * VDIM), bf16),
        in_specs=[anywhere] * 4 + [pl.BlockSpec(memory_space=pltpu.SMEM)],
        out_specs=anywhere,
        scratch_shapes=[
            pltpu.VMEM(queries.shape, bf16),
            pltpu.VMEM((n_head, tokens, heads * WIDTH), bf16),
            pltpu.VMEM((all_tokens, heads * WIDTH), f32),
            pltpu.VMEM(w_uk.shape, bf16),
            pltpu.VMEM(w_uv.shape, bf16),
            pltpu.VMEM((rows, LATENT + ROPE), bf16),
            pltpu.VMEM((chips, 2, LATENT + ROPE, span), bf16),
            pltpu.VMEM((chips, rows, 2 * span), f32),
            pltpu.VMEM((rows, LATENT), f32),
            pltpu.VMEM((all_tokens, heads * VDIM), f32),
            pltpu.VMEM((n_head, tokens, heads * VDIM), bf16),
            dma((6,)),
            dma((n_head,)),
            dma((n_head,)),
            dma((chips,)),
            dma((chips,)),
            dma((chips, 2)),
            dma((n_head,)),
            dma((n_head,)),
        ],
        compiler_params=pltpu.CompilerParams(
            collective_id=0, has_side_effects=True, vmem_limit_bytes=64 * 1024 * 1024 - 64 * 1024
        ),
    )(queries, w_uk, w_uv, latent_cache.T, span_offset)


def solution(mesh):
    return jax.shard_map(
        functools.partial(local, mesh.shape["head"], mesh.shape["ctx"]),
        mesh=mesh,
        in_specs=(
            P(("head", "ctx"), None),
            P("head", None, None),
            P("head", None, None),
            P("ctx", None),
            P(),
        ),
        out_specs=P(("head", "ctx"), None),
        check_vma=False,
    )
```

```python
import functools
import math

import jax
import jax.numpy as jnp
from jax import lax
from jax.experimental import pallas as pl
from jax.experimental.pallas import tpu as pltpu
from jax.sharding import PartitionSpec as P

NOPE = 128
ROPE = 64
LATENT = 512
VDIM = 128
WIDTH = NOPE + ROPE
MESH = pl.DeviceIdType.MESH

yarn_mscale = 0.1 * math.log(40.0) + 1.0
score_scale = WIDTH ** (-0.5) * yarn_mscale**2


def kernel(
    n_head, n_ctx, q_hbm, uk_hbm, uv_hbm, cache_hbm, offset_ref, out_ref,
    q_in, q_got, q_rows, uk, uv, q_all, cache, scores, acc, heads_out, slabs,
    local_sem, q_send, q_recv, own_send, fwd_send, cache_recv, o_send, o_recv,
):
    tokens = q_hbm.shape[0]
    heads = uk_hbm.shape[0]
    span = cache_hbm.shape[1]
    chips = n_ctx // 2
    all_tokens = n_head * tokens
    rows = heads * all_tokens
    q_cols = heads * WIDTH
    o_cols = heads * VDIM
    h_me = lax.axis_index("head")
    c_me = lax.axis_index("ctx")
    chip = c_me // 2
    core = c_me % 2
    sibling = chip * 2 + 1 - core

    def head_peer(i):
        return lax.rem(h_me + i, n_head)

    def chip_peer(i):
        return lax.rem(chip + i, chips)

    def piece(chip_at, core_at):
        return cache.at[chip_at, core_at]

    load_q = pltpu.make_async_copy(q_hbm, q_in, local_sem.at[0])
    load_cache = pltpu.make_async_copy(cache_hbm, piece(chip, core), local_sem.at[1])
    load_uk = pltpu.make_async_copy(uk_hbm, uk, local_sem.at[2])
    load_uv = pltpu.make_async_copy(uv_hbm, uv, local_sem.at[3])
    load_q.start()
    load_cache.start()

    barrier = pltpu.get_barrier_semaphore()
    for i in range(1, n_head):
        pl.semaphore_signal(barrier, inc=1, device_id=(head_peer(i), c_me), device_id_type=MESH)
    for i in range(1, chips):
        pl.semaphore_signal(
            barrier, inc=1, device_id=(h_me, chip_peer(i) * 2 + core), device_id_type=MESH
        )
    pl.semaphore_signal(barrier, inc=1, device_id=(h_me, sibling), device_id_type=MESH)
    load_q.wait()
    load_uk.start()
    load_uv.start()
    pl.semaphore_wait(barrier, n_head - 1 + chips)

    q_copies = []
    for i in range(1, n_head):
        there = head_peer(i)
        copy = pltpu.make_async_remote_copy(
            src_ref=q_in.at[:, pl.ds(pl.multiple_of(there * q_cols, 128), q_cols)],
            dst_ref=q_got.at[h_me],
            send_sem=q_send.at[i],
            recv_sem=q_recv.at[h_me],
            device_id=(there, c_me),
            device_id_type=MESH,
        )
        copy.start()
        q_copies.append(copy)
    load_cache.wait()
    cache_far = []
    for i in range(1, chips):
        there = chip_peer(i)
        copy = pltpu.make_async_remote_copy(
            src_ref=piece(chip, core),
            dst_ref=piece(chip, core),
            send_sem=own_send.at[i],
            recv_sem=cache_recv.at[chip, core],
            device_id=(h_me, there * 2 + core),
            device_id_type=MESH,
        )
        copy.start()
        cache_far.append(copy)
    to_sibling = pltpu.make_async_remote_copy(
        src_ref=piece(chip, core),
        dst_ref=piece(chip, core),
        send_sem=own_send.at[0],
        recv_sem=cache_recv.at[chip, core],
        device_id=(h_me, sibling),
        device_id_type=MESH,
    )
    to_sibling.start()
    own_q = pltpu.make_async_copy(
        q_in.at[:, pl.ds(pl.multiple_of(h_me * q_cols, 128), q_cols)],
        q_got.at[h_me],
        local_sem.at[4],
    )
    own_q.start()
    own_q.wait()

    def arrival(sem, dst, src=None):
        return pltpu.make_async_remote_copy(
            src_ref=dst,
            dst_ref=dst,
            send_sem=sem,
            recv_sem=sem,
            device_id=(h_me, sibling),
            device_id_type=MESH,
        )

    for i in range(1, n_head):
        there = head_peer(i)
        arrival(q_recv.at[there], q_got.at[there]).wait_recv()
    for p in range(n_head):
        q_rows[p * tokens : (p + 1) * tokens, :] = q_got[p].astype(jnp.float32)
    load_uk.wait()
    def to_latent(pair):
        both = q_rows[:, pair * 2 * WIDTH : (pair + 1) * 2 * WIDTH].astype(jnp.bfloat16)
        for k in range(2):
            h = pair * 2 + k
            at = pl.ds(h * all_tokens, all_tokens)
            plain = both[:, k * WIDTH : k * WIDTH + NOPE]
            turned = both[:, k * WIDTH + NOPE : (k + 1) * WIDTH]
            q_all[at, :LATENT] = jnp.dot(
                plain, uk[h], preferred_element_type=jnp.float32
            ).astype(jnp.bfloat16)
            q_all[at, LATENT:] = turned

    pairs = heads // 2
    for pair in range(pairs // 2):
        to_latent(pair)

    forwards = []
    for i in range(1, chips):
        there = chip_peer(i)
        arrival(cache_recv.at[there, core], piece(there, core)).wait_recv()
        copy = pltpu.make_async_remote_copy(
            src_ref=piece(there, core),
            dst_ref=piece(there, core),
            send_sem=fwd_send.at[i],
            recv_sem=cache_recv.at[there, core],
            device_id=(h_me, sibling),
            device_id_type=MESH,
        )
        copy.start()
        forwards.append(copy)

    for pair in range(pairs // 2, pairs):
        to_latent(pair)

    row = lax.broadcasted_iota(jnp.int32, (rows, 1), 0)
    token = lax.rem(row, all_tokens)
    token = (lax.div(token, tokens) * n_ctx + c_me) * tokens + lax.rem(token, tokens)
    query_pos = token + offset_ref[0]
    lane = lax.broadcasted_iota(jnp.int32, (rows, 2 * span), 1)

    def score_step(i, top):
        at = chip_peer(i)
        arrival(cache_recv.at[at, 1 - core], piece(at, 1 - core)).wait_recv()
        keys = jnp.concatenate([cache[at, 0], cache[at, 1]], axis=1)
        s = jnp.dot(q_all[...], keys, preferred_element_type=jnp.float32) * score_scale
        s = jnp.where(lane + at * (2 * span) <= query_pos, s, -jnp.inf)
        scores[at] = s
        return jnp.maximum(top, jnp.max(s, axis=1, keepdims=True))

    unroll = chips if chips <= 4 else 1
    top = lax.fori_loop(
        0, chips, score_step, jnp.full((rows, 1), -jnp.inf, jnp.float32), unroll=unroll
    )
    acc[...] = jnp.zeros_like(acc)

    def value_step(i, total):
        at = chip_peer(i)
        expo = jnp.exp(scores[at] - top)
        values = jnp.concatenate([cache[at, 0, :LATENT], cache[at, 1, :LATENT]], axis=1)
        acc[...] += lax.dot_general(
            expo.astype(jnp.bfloat16),
            values,
            (((1,), (1,)), ((), ())),
            preferred_element_type=jnp.float32,
        )
        return total + jnp.sum(expo, axis=1, keepdims=True)

    total = lax.fori_loop(
        0, chips, value_step, jnp.zeros((rows, 1), jnp.float32), unroll=unroll
    )
    attended = (acc[...] / total).astype(jnp.bfloat16)
    load_uv.wait()
    for h in range(heads):
        heads_out[:, h * VDIM : (h + 1) * VDIM] = jnp.dot(
            attended[h * all_tokens : (h + 1) * all_tokens],
            uv[h],
            preferred_element_type=jnp.float32,
        )
    for p in range(n_head):
        slabs[p] = heads_out[p * tokens : (p + 1) * tokens, :].astype(jnp.bfloat16)

    mine = pl.ds(pl.multiple_of(h_me * o_cols, 128), o_cols)
    out_copies = []
    for i in range(1, n_head):
        there = head_peer(i)
        copy = pltpu.make_async_remote_copy(
            src_ref=slabs.at[there],
            dst_ref=out_ref.at[:, mine],
            send_sem=o_send.at[i],
            recv_sem=o_recv.at[h_me],
            device_id=(there, c_me),
            device_id_type=MESH,
        )
        copy.start()
        out_copies.append(copy)
    own_out = pltpu.make_async_copy(slabs.at[h_me], out_ref.at[:, mine], local_sem.at[5])
    own_out.start()

    for copy in cache_far + q_copies + [to_sibling] + forwards:
        copy.wait_send()
    own_out.wait()
    for i in range(1, n_head):
        there = head_peer(i)
        cols = pl.ds(pl.multiple_of(there * o_cols, 128), o_cols)
        arrival(o_recv.at[there], out_ref.at[:, cols]).wait_recv()
    for copy in out_copies:
        copy.wait_send()


def local(n_head, n_ctx, queries, w_uk, w_uv, latent_cache, span_offset):
    tokens = queries.shape[0]
    heads = w_uk.shape[0]
    span = latent_cache.shape[0]
    chips = n_ctx // 2
    all_tokens = n_head * tokens
    rows = heads * all_tokens
    bf16, f32 = jnp.bfloat16, jnp.float32
    dma = pltpu.SemaphoreType.DMA
    anywhere = pl.BlockSpec(memory_space=pl.ANY)
    return pl.pallas_call(
        functools.partial(kernel, n_head, n_ctx),
        out_shape=jax.ShapeDtypeStruct((tokens, n_head * heads * VDIM), bf16),
        in_specs=[anywhere] * 4 + [pl.BlockSpec(memory_space=pltpu.SMEM)],
        out_specs=anywhere,
        scratch_shapes=[
            pltpu.VMEM(queries.shape, bf16),
            pltpu.VMEM((n_head, tokens, heads * WIDTH), bf16),
            pltpu.VMEM((all_tokens, heads * WIDTH), f32),
            pltpu.VMEM(w_uk.shape, bf16),
            pltpu.VMEM(w_uv.shape, bf16),
            pltpu.VMEM((rows, LATENT + ROPE), bf16),
            pltpu.VMEM((chips, 2, LATENT + ROPE, span), bf16),
            pltpu.VMEM((chips, rows, 2 * span), f32),
            pltpu.VMEM((rows, LATENT), f32),
            pltpu.VMEM((all_tokens, heads * VDIM), f32),
            pltpu.VMEM((n_head, tokens, heads * VDIM), bf16),
            dma((6,)),
            dma((n_head,)),
            dma((n_head,)),
            dma((chips,)),
            dma((chips,)),
            dma((chips, 2)),
            dma((n_head,)),
            dma((n_head,)),
        ],
        compiler_params=pltpu.CompilerParams(
            collective_id=0, has_side_effects=True, vmem_limit_bytes=64 * 1024 * 1024 - 64 * 1024
        ),
    )(queries, w_uk, w_uv, latent_cache.T, span_offset)


def solution(mesh):
    return jax.shard_map(
        functools.partial(local, mesh.shape["head"], mesh.shape["ctx"]),
        mesh=mesh,
        in_specs=(
            P(("head", "ctx"), None),
            P("head", None, None),
            P("head", None, None),
            P("ctx", None),
            P(),
        ),
        out_specs=P(("head", "ctx"), None),
        check_vma=False,
    )
```
